32 devices in a mesh: groups: 2 (over y), expert: 8 (over z, x), tensor: 2 (over core).
Axes of the slice: x: 2, y: 2, z: 4, core: 2. Of those that a mesh axis runs over, the one named last changes fastest.
Arguments:
- tokens: bfloat16 [128, 6144], P(('groups', 'expert'), 'tensor'), parts along dimension 0, may hold values from -6 to 6
- grad_out: bfloat16 [128, 6144], P(('groups', 'expert'), 'tensor'), parts along dimension 0, may hold values from -6 to 6
- gate_weight: bfloat16 [6144, 16384], P('tensor', 'expert'), may hold values from -0.078125 to 0.078125
- up_weight: bfloat16 [6144, 16384], P('tensor', 'expert'), may hold values from -0.078125 to 0.078125
- down_weight: bfloat16 [16384, 6144], P('expert', 'tensor'), may hold values from -0.0625 to 0.0625
- counts: int32 [16, 2], P(('groups', 'expert')), parts along dimension 0, may hold values from 0 to 2, as said below
- slot_token: int32 [16, 2, 2], P(('groups', 'expert')), parts along dimension 0, may hold values from 0 to 7, as said below
- gates: float32 [16, 2, 2], P(('groups', 'expert')), parts along dimension 0, may hold values from 0.25 to 1
Outputs:
- mixed: bfloat16 [128, 6144], P(('groups', 'expert'), 'tensor'), parts along dimension 0
- grad_tokens: bfloat16 [128, 6144], P(('groups', 'expert'), 'tensor'), parts along dimension 0
- grad_gate: bfloat16 [12288, 16384], P(('groups', 'tensor'), 'expert'), parts along dimension 0
- grad_up: bfloat16 [12288, 16384], P(('groups', 'tensor'), 'expert'), parts along dimension 0
- grad_down: bfloat16 [32768, 6144], P(('groups', 'expert'), 'tensor'), parts along dimension 0
The draws below stay inside these ranges and needn't reach their ends.
There are 2 independent parts, one for each index of `groups`. The reference program is written for one: setup_inputs(seed, part) draws one part's arguments, and reference() takes and returns one part's arrays. A program takes and returns all parts, laid end to end along the dimension named above; an argument that names none is the same for every part. Nothing has to cross between parts.
Inputs may be any that keep to these rules, and one draw needn't show every extreme that they name: `counts`: some expert has all 2 slots used by every owner. `slot_token`: the 2 slots of one owner and one expert name distinct tokens.
All inputs are finite; a program needn't handle non-finite values.
Results may differ from the reference program's by a relative error of at most 0.0059.
Values may be sent and summed in bfloat16 or wider, within the bound.
A program may use at most 192 MiB of HBM per device.

```python
import jax
import jax.numpy as jnp
from jax import lax

MODEL_WIDTH = 6144
HIDDEN_WIDTH = 8192
ACTIVE_EXPERTS = 2
SLOT_CAPACITY = 2
TOK_DEV = 8
TOKEN_HOLDERS = 8
TOKENS = 64


def draw_counts(key, part):
    start_offset = jax.random.randint(jax.random.fold_in(key, 11), (TOKEN_HOLDERS, ACTIVE_EXPERTS), 0, SLOT_CAPACITY + 1)
    most_loaded = jax.random.randint(jax.random.fold_in(key, 12), (), 0, ACTIVE_EXPERTS)
    least_loaded = (most_loaded + 1) % ACTIVE_EXPERTS
    column_range = lax.broadcasted_iota(jnp.int32, (TOKEN_HOLDERS, ACTIVE_EXPERTS), 1)
    holder_rows = lax.broadcasted_iota(jnp.int32, (TOKEN_HOLDERS, ACTIVE_EXPERTS), 0)
    start_offset = jnp.where(column_range == most_loaded, SLOT_CAPACITY, start_offset)
    start_offset = jnp.where(holder_rows == 0, SLOT_CAPACITY, start_offset)
    start_offset = jnp.where((holder_rows == 1) & (column_range == least_loaded), 0, start_offset)
    return start_offset.astype(jnp.int32)


def first_tokens(subkey):
    return jax.random.permutation(subkey, TOK_DEV)[:SLOT_CAPACITY]


def draw_slot_token(key, part):
    random_keys = jax.random.split(jax.random.fold_in(key, 21), TOKEN_HOLDERS * ACTIVE_EXPERTS)
    picked_experts = jax.vmap(first_tokens)(random_keys)
    return picked_experts.reshape(TOKEN_HOLDERS, ACTIVE_EXPERTS, SLOT_CAPACITY).astype(jnp.int32)


def block_levels(stream_key, extent, cuts, least, top_value):
    factor_of = 1.0
    for dim, shards_of in cuts:
        draws = jax.random.uniform(jax.random.fold_in(jax.random.fold_in(stream_key, 6), dim), (shards_of,), jnp.float32, least / len(cuts), top_value / len(cuts))
        factor_of = factor_of * jnp.repeat(jnp.exp(draws), extent[dim] // shards_of).reshape((-1,) + (1,) * (len(extent) - 1 - dim))
    return factor_of


def normal_values(rng, dims, width, bound, pieces=(), held_as=jnp.bfloat16):
    gain = block_levels(rng, dims, pieces, -0.22, 0.18) if pieces else 1.0
    entries = jax.random.normal(rng, dims, jnp.float32) * width * gain
    return jnp.minimum(jnp.maximum(entries, -bound), bound).astype(held_as)


def setup_inputs(seed: int = 0, part: int = 0) -> dict:
    key_list = jax.random.split(jax.random.key(seed), 9)
    own_keys = jax.random.split(jax.random.fold_in(key_list[8], part), 9)
    return {
        "tokens": normal_values(own_keys[0], (TOKENS, MODEL_WIDTH), 1.0, 6.0, ((0, 8), (1, 2))),
        "grad_out": normal_values(own_keys[1], (TOKENS, MODEL_WIDTH), 1.0, 6.0, ((0, 8), (1, 2))),
        "gate_weight": normal_values(key_list[2], (MODEL_WIDTH, ACTIVE_EXPERTS * HIDDEN_WIDTH), MODEL_WIDTH ** -0.5, 0.078125, ((0, 2), (1, 8))),
        "up_weight": normal_values(key_list[3], (MODEL_WIDTH, ACTIVE_EXPERTS * HIDDEN_WIDTH), MODEL_WIDTH ** -0.5, 0.078125, ((0, 2), (1, 8))),
        "down_weight": normal_values(key_list[4], (ACTIVE_EXPERTS * HIDDEN_WIDTH, MODEL_WIDTH), HIDDEN_WIDTH ** -0.5, 0.0625, ((0, 8), (1, 2))),
        "counts": draw_counts(jax.random.fold_in(jax.random.fold_in(key_list[8], part), 71), part),
        "slot_token": draw_slot_token(jax.random.fold_in(jax.random.fold_in(key_list[8], part), 71), part),
        "gates": jnp.clip(0.25 + 0.75 * jax.random.uniform(own_keys[7], (TOKEN_HOLDERS, ACTIVE_EXPERTS, SLOT_CAPACITY), jnp.float32) ** block_levels(own_keys[7], (TOKEN_HOLDERS, ACTIVE_EXPERTS, SLOT_CAPACITY), ((0, 8),), -0.2, 0.2), 0.25, 1.0),
    }


def take_rows(source, indices):
    return source[indices]


def add_rows(indices, factor, values):
    return jnp.zeros((TOK_DEV, values.shape[-1]), jnp.float32).at[indices].add(factor[:, None] * values)


def reference(tokens, grad_out, gate_weight, up_weight, down_weight, counts, slot_token, gates):
    holder_devices = counts.shape[0]
    total_slots = ACTIVE_EXPERTS * SLOT_CAPACITY
    tok_rows = tokens.reshape(holder_devices, TOK_DEV, MODEL_WIDTH)
    grad_rows = grad_out.reshape(holder_devices, TOK_DEV, MODEL_WIDTH)
    flat_slots = slot_token.reshape(holder_devices, total_slots).astype(jnp.int32)
    valid_mask = (lax.broadcasted_iota(jnp.int32, (holder_devices, ACTIVE_EXPERTS, SLOT_CAPACITY), 2) < counts[:, :, None]).astype(jnp.float32)
    valid_mask = valid_mask.reshape(holder_devices, total_slots)
    weight = gates.reshape(holder_devices, total_slots) * valid_mask
    picked_x = jax.vmap(take_rows)(tok_rows, flat_slots)
    picked_g = jax.vmap(take_rows)(grad_rows, flat_slots)
    shipped_input = (picked_x.astype(jnp.float32) * valid_mask[:, :, None]).astype(jnp.bfloat16)
    shipped_gradient = (picked_g.astype(jnp.float32) * weight[:, :, None]).astype(jnp.bfloat16)
    shipped_input = shipped_input.reshape(holder_devices, ACTIVE_EXPERTS, SLOT_CAPACITY, MODEL_WIDTH)
    shipped_gradient = shipped_gradient.reshape(holder_devices, ACTIVE_EXPERTS, SLOT_CAPACITY, MODEL_WIDTH)
    out_list = []
    back_list = []
    gate_grads = []
    up_grads = []
    down_grads = []
    for expert_number in range(ACTIVE_EXPERTS):
        rows_x = shipped_input[:, expert_number].reshape(holder_devices * SLOT_CAPACITY, MODEL_WIDTH)
        rows_g = shipped_gradient[:, expert_number].reshape(holder_devices * SLOT_CAPACITY, MODEL_WIDTH)
        gate_cols = gate_weight[:, expert_number * HIDDEN_WIDTH:(expert_number + 1) * HIDDEN_WIDTH]
        up_cols = up_weight[:, expert_number * HIDDEN_WIDTH:(expert_number + 1) * HIDDEN_WIDTH]
        down_rows = down_weight[expert_number * HIDDEN_WIDTH:(expert_number + 1) * HIDDEN_WIDTH]
        pre_gate = jnp.dot(rows_x, gate_cols, preferred_element_type=jnp.float32)
        pre_up = jnp.dot(rows_x, up_cols, preferred_element_type=jnp.float32)
        grad_hidden = jnp.dot(rows_g, down_rows.T, preferred_element_type=jnp.float32)
        gate_sig = jax.nn.sigmoid(pre_gate)
        active = (pre_gate * gate_sig * pre_up).astype(jnp.bfloat16)
        out_slots = jnp.dot(active, down_rows, preferred_element_type=jnp.float32)
        grad_upin = (grad_hidden * pre_gate * gate_sig).astype(jnp.bfloat16)
        grad_gatein = (grad_hidden * pre_up * gate_sig * (1.0 + pre_gate * (1.0 - gate_sig))).astype(jnp.bfloat16)
        back_slots = jnp.dot(grad_gatein, gate_cols.T, preferred_element_type=jnp.float32) + jnp.dot(grad_upin, up_cols.T, preferred_element_type=jnp.float32)
        gate_grads.append(jnp.dot(rows_x.T, grad_gatein, preferred_element_type=jnp.float32).astype(jnp.bfloat16))
        up_grads.append(jnp.dot(rows_x.T, grad_upin, preferred_element_type=jnp.float32).astype(jnp.bfloat16))
        down_grads.append(jnp.dot(active.T, rows_g, preferred_element_type=jnp.float32).astype(jnp.bfloat16))
        out_list.append(out_slots.reshape(holder_devices, SLOT_CAPACITY, MODEL_WIDTH))
        back_list.append(back_slots.reshape(holder_devices, SLOT_CAPACITY, MODEL_WIDTH))
    out_all = jnp.stack(out_list, axis=1).reshape(holder_devices, total_slots, MODEL_WIDTH)
    back_all = jnp.stack(back_list, axis=1).reshape(holder_devices, total_slots, MODEL_WIDTH)
    mixed = jax.vmap(add_rows)(flat_slots, weight, out_all).reshape(holder_devices * TOK_DEV, MODEL_WIDTH).astype(jnp.bfloat16)
    grad_tokens = jax.vmap(add_rows)(flat_slots, valid_mask, back_all).reshape(holder_devices * TOK_DEV, MODEL_WIDTH).astype(jnp.bfloat16)
    grad_gate = jnp.concatenate(gate_grads, axis=1)
    grad_up = jnp.concatenate(up_grads, axis=1)
    grad_down = jnp.concatenate(down_grads, axis=0)
    return (mixed, grad_tokens, grad_gate, grad_up, grad_down)
```

```python
import functools

import jax
import jax.numpy as jnp
from jax import lax
from jax.experimental import pallas as pl
from jax.experimental.pallas import tpu as pltpu
from jax.sharding import PartitionSpec as P

MESH = pl.DeviceIdType.MESH
F32 = jnp.float32
BF16 = jnp.bfloat16

EXPERTS = 2
SLOTS = 2
PIECES = 8
RPIECES = 4
RCHUNK = 512


def iota(shape, dim):
    return lax.broadcasted_iota(jnp.int32, shape, dim)


def nn(a, b):
    return jnp.dot(a, b, preferred_element_type=F32)


def nt(a, b):
    return lax.dot_general(a, b, (((1,), (1,)), ((), ())), preferred_element_type=F32)


def tn(a, b):
    return lax.dot_general(a, b, (((0,), (0,)), ((), ())), preferred_element_type=F32)


def layer_kernel(
    n, hl, hc, tok, go, wg, wu, wd, counts, slot, gates,
    xr, gr, act, dup, dgt, mixed, gtok,
    wgv, wuv, wdv, sendx, sendg, landx, landg, gus, gur, ps, pr, rets, retl,
    wgsem, wusem, wdsem, xs, xv, gs, gv, guss, gurs, pss, prs, rss, rrs,
):
    me = lax.axis_index("expert")
    other = 1 - lax.axis_index("tensor")
    sub = n // EXPERTS
    rows = n * SLOTS
    width = tok.shape[1]
    tok_dev = tok.shape[0]
    nch = hl // hc
    nd = width // RCHUNK
    piece = width // PIECES
    rl = RCHUNK // RPIECES

    def load(hbm, vmem, sem, c, axis):
        at = pl.ds(pl.multiple_of(c * hc, hc), hc)
        view = (slice(None), at) if axis == 1 else (at, slice(None))
        return pltpu.make_async_copy(hbm.at[view], vmem.at[view], sem.at[c])

    @pl.loop(0, nch)
    def _(c):
        load(wg, wgv, wgsem, c, 1).start()
        load(wu, wuv, wusem, c, 1).start()

    @pl.loop(0, nch)
    def _(c):
        load(wd, wdv, wdsem, c, 0).start()

    barrier = pltpu.get_barrier_semaphore()

    @pl.loop(1, n)
    def _(i):
        pl.semaphore_signal(
            barrier, inc=1, device_id={"expert": lax.rem(me + i, n)}, device_id_type=MESH
        )

    pl.semaphore_signal(barrier, inc=1, device_id={"tensor": other}, device_id_type=MESH)

    srows = EXPERTS * SLOTS * PIECES
    r_i = iota((srows, tok_dev), 0)
    t_i = iota((srows, tok_dev), 1)
    pick = jnp.zeros((srows, tok_dev), F32)
    r_c = iota((srows, 1), 0)
    scale = jnp.zeros((srows, 1), F32)
    for e in range(EXPERTS):
        for s in range(SLOTS):
            q = e * SLOTS + s
            live = jnp.where(s < counts[0, e], 1.0, 0.0).astype(F32)
            pick = jnp.where((r_i // PIECES == q) & (t_i == slot[0, e, s]), live, pick)
            scale = jnp.where(r_c // PIECES == q, gates[0, e, s], scale)
    xa = jnp.zeros((srows, piece), F32)
    ga = jnp.zeros((srows, piece), F32)
    for k in range(PIECES):
        pk = jnp.where(r_i % PIECES == k, pick, 0.0).astype(BF16)
        xa = xa + nn(pk, tok[:, k * piece : (k + 1) * piece])
        ga = ga + nn(pk, go[:, k * piece : (k + 1) * piece])
    ga = ga * scale
    for e in range(EXPERTS):
        sendx[e] = xa[e * 16 : (e + 1) * 16].astype(BF16)
        sendg[e] = ga[e * 16 : (e + 1) * 16].astype(BF16)

    pl.semaphore_wait(barrier, n)

    def dispatch(buf, land, ssem, rsem, i, sending):
        peer = lax.rem(me + i, n)
        at = me if sending else peer
        return pltpu.make_async_remote_copy(
            src_ref=buf.at[peer // sub],
            dst_ref=land.at[at],
            send_sem=ssem.at[peer],
            recv_sem=rsem.at[at],
            device_id={"expert": peer},
            device_id_type=MESH,
        )

    @pl.loop(1, n)
    def _(i):
        dispatch(sendx, landx, xs, xv, i, True).start()

    @pl.loop(1, n)
    def _(i):
        dispatch(sendg, landg, gs, gv, i, True).start()

    landx[me] = sendx[me // sub]
    landg[me] = sendg[me // sub]

    d_r = iota((rows, n * 16), 0)
    d_c = iota((rows, n * 16), 1)

    def unpack(land, out):
        flat = land[...].reshape(n * 16, piece)
        for k in range(PIECES):
            sel = jnp.where(d_c == d_r * PIECES + k, 1.0, 0.0).astype(BF16)
            out[:, k * piece : (k + 1) * piece] = nn(sel, flat).astype(BF16)

    @pl.loop(1, n)
    def _(i):
        dispatch(sendx, landx, xs, xv, i, False).wait_recv()

    unpack(landx, xr)

    def swap(buf, land, ssem, rsem, c):
        return pltpu.make_async_remote_copy(
            src_ref=buf.at[c],
            dst_ref=land.at[c],
            send_sem=ssem.at[c],
            recv_sem=rsem.at[c],
            device_id={"tensor": other},
            device_id_type=MESH,
        )

    @pl.loop(0, nch)
    def _(c):
        at = pl.ds(pl.multiple_of(c * hc, hc), hc)
        load(wg, wgv, wgsem, c, 1).wait()
        gus[c, 0] = nn(xr[...], wgv[:, at])
        load(wu, wuv, wusem, c, 1).wait()
        gus[c, 1] = nn(xr[...], wuv[:, at])
        swap(gus, gur, guss, gurs, c).start()

    @pl.loop(1, n)
    def _(i):
        dispatch(sendg, landg, gs, gv, i, False).wait_recv()

    unpack(landg, gr)

    @pl.loop(0, nch)
    def _(c):
        at = pl.ds(pl.multiple_of(c * hc, hc), hc)
        load(wd, wdv, wdsem, c, 0).wait()
        ps[c] = nt(gr[...], wdv[at, :])
        swap(ps, pr, pss, prs, c).start()

    @pl.loop(0, nch)
    def _(c):
        at = pl.ds(pl.multiple_of(c * hc, hc), hc)
        swap(gus, gur, guss, gurs, c).wait_recv()
        swap(ps, pr, pss, prs, c).wait_recv()
        g = gus[c, 0] + gur[c, 0]
        u = gus[c, 1] + gur[c, 1]
        p = ps[c] + pr[c]
        sig = jax.nn.sigmoid(g)
        gsig = g * sig
        act[:, at] = (gsig * u).astype(BF16)
        dup[:, at] = (p * gsig).astype(BF16)
        dgt[:, at] = (p * u * sig * (1.0 + g * (1.0 - sig))).astype(BF16)

    m_r = iota((n * 16, rows), 0)
    m_c = iota((n * 16, rows), 1)
    home = (m_r // 16) * SLOTS + (m_r // RPIECES) % SLOTS == m_c

    def back(j, i, sending):
        peer = lax.rem(me + i, n)
        at = me if sending else peer
        return pltpu.make_async_remote_copy(
            src_ref=rets.at[j, peer],
            dst_ref=retl.at[j, at],
            send_sem=rss.at[j, peer],
            recv_sem=rrs.at[j, at],
            device_id={"expert": peer},
            device_id_type=MESH,
        )

    @pl.loop(0, nd)
    def _(j):
        at = pl.ds(pl.multiple_of(j * RCHUNK, RCHUNK), RCHUNK)
        y = nn(act[...], wdv[:, at])
        dx = nt(dgt[...], wgv[at, :]) + nt(dup[...], wuv[at, :])
        total = jnp.zeros((n * 16, rl), F32)
        for arr, val in ((0, y.astype(BF16)), (1, dx.astype(BF16))):
            for k in range(RPIECES):
                here = home & ((m_r // 8) % 2 == arr) & (m_r % RPIECES == k)
                sel = jnp.where(here, 1.0, 0.0).astype(BF16)
                total = total + nn(sel, val[:, k * rl : (k + 1) * rl])
        rets[j] = total.astype(BF16).reshape(n, 16, rl)

        @pl.loop(1, n)
        def _(i):
            back(j, i, True).start()

        retl[j, me] = rets[j, me]

    tcol = iota((tok_dev, 1), 0)
    weights = []
    for e in range(EXPERTS):
        for s in range(SLOTS):
            live = jnp.where(s < counts[0, e], 1.0, 0.0).astype(F32)
            hit = jnp.where(tcol == slot[0, e, s], live, 0.0)
            weights.append((hit * gates[0, e, s], hit))

    @pl.loop(0, nd)
    def _(j):
        @pl.loop(1, n)
        def _(i):
            back(j, i, False).wait_recv()

        sums = []
        for e in range(EXPERTS):
            sums.append(
                lax.fori_loop(
                    1,
                    sub,
                    lambda d, acc: acc + retl[j, e * sub + d].astype(F32),
                    retl[j, e * sub].astype(F32),
                )
            )
        for arr, out in ((0, mixed), (1, gtok)):
            for k in range(RPIECES):
                acc = jnp.zeros((tok_dev, rl), F32)
                for e in range(EXPERTS):
                    for s in range(SLOTS):
                        row = arr * 8 + s * RPIECES + k
                        acc = acc + weights[e * SLOTS + s][arr] * sums[e][row : row + 1, :]
                out[:, pl.ds(pl.multiple_of(j * RCHUNK + k * rl, rl), rl)] = acc

    @pl.loop(1, n)
    def _(i):
        dispatch(sendx, landx, xs, xv, i, True).wait_send()
        dispatch(sendg, landg, gs, gv, i, True).wait_send()

        @pl.loop(0, nd)
        def _(j):
            back(j, i, True).wait_send()

    @pl.loop(0, nch)
    def _(c):
        swap(gus, gur, guss, gurs, c).wait_send()
        swap(ps, pr, pss, prs, c).wait_send()


def layer(n, tokens, grad_out, wg, wu, wd, counts, slot, gates):
    tok_dev, width = tokens.shape
    hl = wg.shape[1]
    hc = min(256, hl)
    nch = hl // hc
    rows = n * SLOTS
    nd = width // RCHUNK
    rl = RCHUNK // RPIECES
    piece = width // PIECES
    vmem = pl.BlockSpec(memory_space=pltpu.VMEM)
    smem = pl.BlockSpec(memory_space=pltpu.SMEM)
    hbm = pl.BlockSpec(memory_space=pl.ANY)
    dma = pltpu.SemaphoreType.DMA
    return pl.pallas_call(
        functools.partial(layer_kernel, n, hl, hc),
        out_shape=(
            jax.ShapeDtypeStruct((rows, width), BF16),
            jax.ShapeDtypeStruct((rows, width), BF16),
            jax.ShapeDtypeStruct((rows, hl), BF16),
            jax.ShapeDtypeStruct((rows, hl), BF16),
            jax.ShapeDtypeStruct((rows, hl), BF16),
            jax.ShapeDtypeStruct((tok_dev, width), F32),
            jax.ShapeDtypeStruct((tok_dev, width), F32),
        ),
        in_specs=[vmem, vmem, hbm, hbm, hbm, smem, smem, smem],
        out_specs=(vmem,) * 7,
        scratch_shapes=[
            pltpu.VMEM((width, hl), BF16),
            pltpu.VMEM((width, hl), BF16),
            pltpu.VMEM((hl, width), BF16),
            pltpu.VMEM((EXPERTS, 16, piece), BF16),
            pltpu.VMEM((EXPERTS, 16, piece), BF16),
            pltpu.VMEM((n, 16, piece), BF16),
            pltpu.VMEM((n, 16, piece), BF16),
            pltpu.VMEM((nch, 2, rows, hc), F32),
            pltpu.VMEM((nch, 2, rows, hc), F32),
            pltpu.VMEM((nch, rows, hc), F32),
            pltpu.VMEM((nch, rows, hc), F32),
            pltpu.VMEM((nd, n, 16, rl), BF16),
            pltpu.VMEM((nd, n, 16, rl), BF16),
            dma((nch,)), dma((nch,)), dma((nch,)),
            dma((n,)), dma((n,)), dma((n,)), dma((n,)),
            dma((nch,)), dma((nch,)), dma((nch,)), dma((nch,)),
            dma((nd, n)), dma((nd, n)),
        ],
        compiler_params=pltpu.CompilerParams(
            collective_id=0, has_side_effects=True, vmem_limit_bytes=58 * 1024 * 1024
        ),
        name="layer",
    )(tokens, grad_out, wg, wu, wd, counts, slot, gates)


def grads_kernel(step_h, xr, gr, act, dup, dgt, mixed, gtok, m_out, t_out, gg, gu, gd):
    @pl.when(pl.program_id(0) == 0)
    def _():
        m_out[...] = mixed[...].astype(BF16)
        t_out[...] = gtok[...].astype(BF16)

    hl = dup.shape[1]
    x = xr[...]
    q = gr[...]
    for h in range(0, hl, step_h):
        gg[:, h : h + step_h] = tn(x, dgt[:, h : h + step_h]).astype(BF16)
        gu[:, h : h + step_h] = tn(x, dup[:, h : h + step_h]).astype(BF16)
        gd[h : h + step_h, :] = tn(act[:, h : h + step_h], q).astype(BF16)


def weight_grads(xr, gr, act, dup, dgt, mixed, gtok):
    rows, width = xr.shape
    hl = act.shape[1]
    tok_dev = mixed.shape[0]
    steps = 8
    dw = width // steps
    cols = pl.BlockSpec((rows, dw), lambda i: (0, i))
    hid = pl.BlockSpec((rows, hl), lambda i: (0, 0))
    small = pl.BlockSpec((tok_dev, width), lambda i: (0, 0))
    return pl.pallas_call(
        functools.partial(grads_kernel, min(256, hl)),
        grid=(steps,),
        out_shape=(
            jax.ShapeDtypeStruct((tok_dev, width), BF16),
            jax.ShapeDtypeStruct((tok_dev, width), BF16),
            jax.ShapeDtypeStruct((width, hl), BF16),
            jax.ShapeDtypeStruct((width, hl), BF16),
            jax.ShapeDtypeStruct((hl, width), BF16),
        ),
        in_specs=[cols, cols, hid, hid, hid, small, small],
        out_specs=(
            small,
            small,
            pl.BlockSpec((dw, hl), lambda i: (i, 0)),
            pl.BlockSpec((dw, hl), lambda i: (i, 0)),
            pl.BlockSpec((hl, dw), lambda i: (0, i)),
        ),
        compiler_params=pltpu.CompilerParams(
            dimension_semantics=("arbitrary",), vmem_limit_bytes=48 * 1024 * 1024
        ),
        name="weight_grads",
    )(xr, gr, act, dup, dgt, mixed, gtok)


def shards(tokens, grad_out, gate_weight, up_weight, down_weight, counts, slot_token, gates):
    n = lax.axis_size("expert")
    held = layer(
        n, tokens, grad_out, gate_weight, up_weight, down_weight, counts, slot_token, gates
    )
    return weight_grads(*held)


def solution(mesh):
    in_specs = (
        P(("groups", "expert"), "tensor"),
        P(("groups", "expert"), "tensor"),
        P("tensor", "expert"),
        P("tensor", "expert"),
        P("expert", "tensor"),
        P(("groups", "expert"), None),
        P(("groups", "expert"), None, None),
        P(("groups", "expert"), None, None),
    )
    out_specs = (
        P(("groups", "expert"), "tensor"),
        P(("groups", "expert"), "tensor"),
        P(("groups", "tensor"), "expert"),
        P(("groups", "tensor"), "expert"),
        P(("groups", "expert"), "tensor"),
    )
    return jax.shard_map(shards, mesh=mesh, in_specs=in_specs, out_specs=out_specs, check_vma=False)
```

```python
import functools

import jax
import jax.numpy as jnp
from jax import lax
from jax.experimental import pallas as pl
from jax.experimental.pallas import tpu as pltpu
from jax.sharding import PartitionSpec as P

MESH = pl.DeviceIdType.MESH
F32 = jnp.float32
BF16 = jnp.bfloat16

EXPERTS = 2
SLOTS = 2
PIECES = 8
RPIECES = 4
RCHUNK = 512


def iota(shape, dim):
    return lax.broadcasted_iota(jnp.int32, shape, dim)


def nn(a, b):
    return jnp.dot(a, b, preferred_element_type=F32)


def nt(a, b):
    return lax.dot_general(a, b, (((1,), (1,)), ((), ())), preferred_element_type=F32)


def tn(a, b):
    return lax.dot_general(a, b, (((0,), (0,)), ((), ())), preferred_element_type=F32)


def layer_kernel(
    n, hl, hc, tok, go, wg, wu, wd, counts, slot, gates,
    xr, gr, act, dup, dgt, mixed, gtok,
    wgv, wuv, wdv, home, sendx, sendg, landx, landg, gus, gur, ps, pr, rets, retl,
    wgsem, wusem, wdsem, xs, xv, gs, gv, guss, gurs, pss, prs, rss, rrs,
):
    me = lax.axis_index("expert")
    other = 1 - lax.axis_index("tensor")
    sub = n // EXPERTS
    rows = n * SLOTS
    width = tok.shape[1]
    tok_dev = tok.shape[0]
    nch = hl // hc
    nd = width // RCHUNK
    piece = width // PIECES
    rl = RCHUNK // RPIECES

    def load(hbm, vmem, sem, c, axis):
        at = pl.ds(pl.multiple_of(c * hc, hc), hc)
        view = (slice(None), at) if axis == 1 else (at, slice(None))
        return pltpu.make_async_copy(hbm.at[view], vmem.at[view], sem.at[c])

    @pl.loop(0, nch)
    def _(c):
        load(wg, wgv, wgsem, c, 1).start()
        load(wu, wuv, wusem, c, 1).start()

    @pl.loop(0, nch)
    def _(c):
        load(wd, wdv, wdsem, c, 0).start()

    barrier = pltpu.get_barrier_semaphore()

    @pl.loop(1, n)
    def _(i):
        pl.semaphore_signal(
            barrier, inc=1, device_id={"expert": lax.rem(me + i, n)}, device_id_type=MESH
        )

    pl.semaphore_signal(barrier, inc=1, device_id={"tensor": other}, device_id_type=MESH)

    srows = EXPERTS * SLOTS * PIECES
    r_i = iota((srows, PIECES * tok_dev), 0)
    c_i = iota((srows, PIECES * tok_dev), 1)
    same = r_i % PIECES == c_i // tok_dev
    pick = jnp.zeros((srows, PIECES * tok_dev), F32)
    r_c = iota((srows, 1), 0)
    scale = jnp.zeros((srows, 1), F32)
    for e in range(EXPERTS):
        for s in range(SLOTS):
            q = e * SLOTS + s
            live = jnp.where(s < counts[0, e], 1.0, 0.0).astype(F32)
            hit = same & (r_i // PIECES == q) & (c_i % tok_dev == slot[0, e, s])
            pick = jnp.where(hit, live, pick)
            scale = jnp.where(r_c // PIECES == q, gates[0, e, s], scale)
    pick = pick.astype(BF16)

    def stack(ref):
        wide = ref[...].astype(F32)
        parts = [wide[:, k * piece : (k + 1) * piece] for k in range(PIECES)]
        return jnp.concatenate(parts, axis=0).astype(BF16)

    xa = nn(pick, stack(tok))
    ga = nn(pick, stack(go))
    ga = ga * scale
    for e in range(EXPERTS):
        sendx[e] = xa[e * 16 : (e + 1) * 16].astype(BF16)
        sendg[e] = ga[e * 16 : (e + 1) * 16].astype(BF16)

    pl.semaphore_wait(barrier, n)

    def dispatch(buf, land, ssem, rsem, i, sending):
        peer = lax.rem(me + i, n)
        at = me if sending else peer
        return pltpu.make_async_remote_copy(
            src_ref=buf.at[peer // sub],
            dst_ref=land.at[at],
            send_sem=ssem.at[peer],
            recv_sem=rsem.at[at],
            device_id={"expert": peer},
            device_id_type=MESH,
        )

    @pl.loop(1, n)
    def _(i):
        dispatch(sendx, landx, xs, xv, i, True).start()

    @pl.loop(1, n)
    def _(i):
        dispatch(sendg, landg, gs, gv, i, True).start()

    landx[me] = sendx[me // sub]
    landg[me] = sendg[me // sub]

    d_r = iota((PIECES * rows, n * 16), 0)
    d_c = iota((PIECES * rows, n * 16), 1)
    spread = (d_c == (d_r % rows) * PIECES + d_r // rows).astype(F32).astype(BF16)
    m_r = iota((n * 16, 2 * RPIECES * rows), 0)
    m_c = iota((n * 16, 2 * RPIECES * rows), 1)
    m_row = (m_r // 16) * SLOTS + (m_r // RPIECES) % SLOTS
    m_part = ((m_r // 8) % 2) * RPIECES + m_r % RPIECES
    home[...] = (m_c == m_part * rows + m_row).astype(F32).astype(BF16)

    def unpack(land, out):
        moved = nn(spread, land[...].reshape(n * 16, piece)).astype(BF16)
        for k in range(PIECES):
            out[:, k * piece : (k + 1) * piece] = moved[k * rows : (k + 1) * rows]

    @pl.loop(1, n)
    def _(i):
        dispatch(sendx, landx, xs, xv, i, False).wait_recv()

    unpack(landx, xr)

    def swap(buf, land, ssem, rsem, c):
        return pltpu.make_async_remote_copy(
            src_ref=buf.at[c],
            dst_ref=land.at[c],
            send_sem=ssem.at[c],
            recv_sem=rsem.at[c],
            device_id={"tensor": other},
            device_id_type=MESH,
        )

    @pl.loop(0, nch)
    def _(c):
        at = pl.ds(pl.multiple_of(c * hc, hc), hc)
        load(wg, wgv, wgsem, c, 1).wait()
        gus[c, 0] = nn(xr[...], wgv[:, at])
        load(wu, wuv, wusem, c, 1).wait()
        gus[c, 1] = nn(xr[...], wuv[:, at])
        swap(gus, gur, guss, gurs, c).start()

    @pl.loop(1, n)
    def _(i):
        dispatch(sendg, landg, gs, gv, i, False).wait_recv()

    unpack(landg, gr)

    @pl.loop(0, nch)
    def _(c):
        at = pl.ds(pl.multiple_of(c * hc, hc), hc)
        load(wd, wdv, wdsem, c, 0).wait()
        ps[c] = nt(gr[...], wdv[at, :])
        swap(ps, pr, pss, prs, c).start()

    @pl.loop(0, nch)
    def _(c):
        at = pl.ds(pl.multiple_of(c * hc, hc), hc)
        swap(gus, gur, guss, gurs, c).wait_recv()
        swap(ps, pr, pss, prs, c).wait_recv()
        g = gus[c, 0] + gur[c, 0]
        u = gus[c, 1] + gur[c, 1]
        p = ps[c] + pr[c]
        sig = jax.nn.sigmoid(g)
        gsig = g * sig
        act[:, at] = (gsig * u).astype(BF16)
        dup[:, at] = (p * gsig).astype(BF16)
        dgt[:, at] = (p * u * sig * (1.0 + g * (1.0 - sig))).astype(BF16)

    def back(j, i, sending):
        peer = lax.rem(me + i, n)
        at = me if sending else peer
        return pltpu.make_async_remote_copy(
            src_ref=rets.at[j, peer],
            dst_ref=retl.at[j, at],
            send_sem=rss.at[j, peer],
            recv_sem=rrs.at[j, at],
            device_id={"expert": peer},
            device_id_type=MESH,
        )

    @pl.loop(0, nd)
    def _(j):
        at = pl.ds(pl.multiple_of(j * RCHUNK, RCHUNK), RCHUNK)
        y = nn(act[...], wdv[:, at])
        dx = nt(dgt[...], wgv[at, :]) + nt(dup[...], wuv[at, :])
        vals = (y.astype(BF16), dx.astype(BF16))
        parts = [v[:, k * rl : (k + 1) * rl] for v in vals for k in range(RPIECES)]
        total = nn(home[...], jnp.concatenate(parts, axis=0))
        rets[j] = total.astype(BF16).reshape(n, 16, rl)

        @pl.loop(1, n)
        def _(i):
            back(j, i, True).start()

        retl[j, me] = rets[j, me]

    tcol = iota((tok_dev, 1), 0)
    weights = []
    for e in range(EXPERTS):
        for s in range(SLOTS):
            live = jnp.where(s < counts[0, e], 1.0, 0.0).astype(F32)
            hit = jnp.where(tcol == slot[0, e, s], live, 0.0)
            weights.append((hit * gates[0, e, s], hit))

    @pl.loop(0, nd)
    def _(j):
        @pl.loop(1, n)
        def _(i):
            back(j, i, False).wait_recv()

        sums = []
        for e in range(EXPERTS):
            sums.append(
                lax.fori_loop(
                    1,
                    sub,
                    lambda d, acc: acc + retl[j, e * sub + d].astype(F32),
                    retl[j, e * sub].astype(F32),
                )
            )
        for arr, out in ((0, mixed), (1, gtok)):
            for k in range(RPIECES):
                acc = jnp.zeros((tok_dev, rl), F32)
                for e in range(EXPERTS):
                    for s in range(SLOTS):
                        row = arr * 8 + s * RPIECES + k
                        acc = acc + weights[e * SLOTS + s][arr] * sums[e][row : row + 1, :]
                out[:, pl.ds(pl.multiple_of(j * RCHUNK + k * rl, rl), rl)] = acc

    @pl.loop(1, n)
    def _(i):
        dispatch(sendx, landx, xs, xv, i, True).wait_send()
        dispatch(sendg, landg, gs, gv, i, True).wait_send()

        @pl.loop(0, nd)
        def _(j):
            back(j, i, True).wait_send()

    @pl.loop(0, nch)
    def _(c):
        swap(gus, gur, guss, gurs, c).wait_send()
        swap(ps, pr, pss, prs, c).wait_send()


def layer(n, tokens, grad_out, wg, wu, wd, counts, slot, gates):
    tok_dev, width = tokens.shape
    hl = wg.shape[1]
    hc = min(512, hl)
    nch = hl // hc
    rows = n * SLOTS
    nd = width // RCHUNK
    rl = RCHUNK // RPIECES
    piece = width // PIECES
    vmem = pl.BlockSpec(memory_space=pltpu.VMEM)
    smem = pl.BlockSpec(memory_space=pltpu.SMEM)
    hbm = pl.BlockSpec(memory_space=pl.ANY)
    dma = pltpu.SemaphoreType.DMA
    return pl.pallas_call(
        functools.partial(layer_kernel, n, hl, hc),
        out_shape=(
            jax.ShapeDtypeStruct((rows, width), BF16),
            jax.ShapeDtypeStruct((rows, width), BF16),
            jax.ShapeDtypeStruct((rows, hl), BF16),
            jax.ShapeDtypeStruct((rows, hl), BF16),
            jax.ShapeDtypeStruct((rows, hl), BF16),
            jax.ShapeDtypeStruct((tok_dev, width), F32),
            jax.ShapeDtypeStruct((tok_dev, width), F32),
        ),
        in_specs=[vmem, vmem, hbm, hbm, hbm, smem, smem, smem],
        out_specs=(vmem,) * 7,
        scratch_shapes=[
            pltpu.VMEM((width, hl), BF16),
            pltpu.VMEM((width, hl), BF16),
            pltpu.VMEM((hl, width), BF16),
            pltpu.VMEM((n * 16, 2 * RPIECES * rows), BF16),
            pltpu.VMEM((EXPERTS, 16, piece), BF16),
            pltpu.VMEM((EXPERTS, 16, piece), BF16),
            pltpu.VMEM((n, 16, piece), BF16),
            pltpu.VMEM((n, 16, piece), BF16),
            pltpu.VMEM((nch, 2, rows, hc), F32),
            pltpu.VMEM((nch, 2, rows, hc), F32),
            pltpu.VMEM((nch, rows, hc), F32),
            pltpu.VMEM((nch, rows, hc), F32),
            pltpu.VMEM((nd, n, 16, rl), BF16),
            pltpu.VMEM((nd, n, 16, rl), BF16),
            dma((nch,)), dma((nch,)), dma((nch,)),
            dma((n,)), dma((n,)), dma((n,)), dma((n,)),
            dma((nch,)), dma((nch,)), dma((nch,)), dma((nch,)),
            dma((nd, n)), dma((nd, n)),
        ],
        compiler_params=pltpu.CompilerParams(
            collective_id=0, has_side_effects=True, vmem_limit_bytes=58 * 1024 * 1024
        ),
        name="layer",
    )(tokens, grad_out, wg, wu, wd, counts, slot, gates)


def grads_kernel(step_h, xr, gr, act, dup, dgt, mixed, gtok, m_out, t_out, gg, gu, gd):
    @pl.when(pl.program_id(0) == 0)
    def _():
        m_out[...] = mixed[...].astype(BF16)
        t_out[...] = gtok[...].astype(BF16)

    hl = dup.shape[1]
    x = xr[...]
    q = gr[...]
    for h in range(0, hl, step_h):
        gg[:, h : h + step_h] = tn(x, dgt[:, h : h + step_h]).astype(BF16)
        gu[:, h : h + step_h] = tn(x, dup[:, h : h + step_h]).astype(BF16)
        gd[h : h + step_h, :] = tn(act[:, h : h + step_h], q).astype(BF16)


def weight_grads(xr, gr, act, dup, dgt, mixed, gtok):
    rows, width = xr.shape
    hl = act.shape[1]
    tok_dev = mixed.shape[0]
    steps = 8
    dw = width // steps
    cols = pl.BlockSpec((rows, dw), lambda i: (0, i))
    hid = pl.BlockSpec((rows, hl), lambda i: (0, 0))
    small = pl.BlockSpec((tok_dev, width), lambda i: (0, 0))
    return pl.pallas_call(
        functools.partial(grads_kernel, min(256, hl)),
        grid=(steps,),
        out_shape=(
            jax.ShapeDtypeStruct((tok_dev, width), BF16),
            jax.ShapeDtypeStruct((tok_dev, width), BF16),
            jax.ShapeDtypeStruct((width, hl), BF16),
            jax.ShapeDtypeStruct((width, hl), BF16),
            jax.ShapeDtypeStruct((hl, width), BF16),
        ),
        in_specs=[cols, cols, hid, hid, hid, small, small],
        out_specs=(
            small,
            small,
            pl.BlockSpec((dw, hl), lambda i: (i, 0)),
            pl.BlockSpec((dw, hl), lambda i: (i, 0)),
            pl.BlockSpec((hl, dw), lambda i: (0, i)),
        ),
        compiler_params=pltpu.CompilerParams(
            dimension_semantics=("arbitrary",), vmem_limit_bytes=60 * 1024 * 1024
        ),
        name="weight_grads",
    )(xr, gr, act, dup, dgt, mixed, gtok)


def shards(tokens, grad_out, gate_weight, up_weight, down_weight, counts, slot_token, gates):
    n = lax.axis_size("expert")
    held = layer(
        n, tokens, grad_out, gate_weight, up_weight, down_weight, counts, slot_token, gates
    )
    return weight_grads(*held)


def solution(mesh):
    in_specs = (
        P(("groups", "expert"), "tensor"),
        P(("groups", "expert"), "tensor"),
        P("tensor", "expert"),
        P("tensor", "expert"),
        P("expert", "tensor"),
        P(("groups", "expert"), None),
        P(("groups", "expert"), None, None),
        P(("groups", "expert"), None, None),
    )
    out_specs = (
        P(("groups", "expert"), "tensor"),
        P(("groups", "expert"), "tensor"),
        P(("groups", "tensor"), "expert"),
        P(("groups", "tensor"), "expert"),
        P(("groups", "expert"), "tensor"),
    )
    return jax.shard_map(shards, mesh=mesh, in_specs=in_specs, out_specs=out_specs, check_vma=False)
```

```python
import functools

import jax
import jax.numpy as jnp
from jax import lax
from jax.experimental import pallas as pl
from jax.experimental.pallas import tpu as pltpu
from jax.sharding import PartitionSpec as P

MESH = pl.DeviceIdType.MESH
F32 = jnp.float32
BF16 = jnp.bfloat16

EXPERTS = 2
SLOTS = 2
PIECES = 8
RPIECES = 4
RCHUNK = 1024


def iota(shape, dim):
    return lax.broadcasted_iota(jnp.int32, shape, dim)


def nn(a, b):
    return jnp.dot(a, b, preferred_element_type=F32)


def nt(a, b):
    return lax.dot_general(a, b, (((1,), (1,)), ((), ())), preferred_element_type=F32)


def tn(a, b):
    return lax.dot_general(a, b, (((0,), (0,)), ((), ())), preferred_element_type=F32)


def layer_kernel(
    n, hl, hc, tok, go, wg, wu, wd, counts, slot, gates,
    xr, gr, act, dup, dgt, mixed, gtok,
    wgv, wuv, wdv, home, sendx, sendg, landx, landg, gus, gur, ps, pr, rets, retl,
    wgsem, wusem, wdsem, xs, xv, gs, gv, guss, gurs, pss, prs, rss, rrs,
):
    me = lax.axis_index("expert")
    other = 1 - lax.axis_index("tensor")
    sub = n // EXPERTS
    rows = n * SLOTS
    width = tok.shape[1]
    tok_dev = tok.shape[0]
    nch = hl // hc
    nd = width // RCHUNK
    piece = width // PIECES
    rl = RCHUNK // RPIECES

    def load(hbm, vmem, sem, c, axis):
        at = pl.ds(pl.multiple_of(c * hc, hc), hc)
        view = (slice(None), at) if axis == 1 else (at, slice(None))
        return pltpu.make_async_copy(hbm.at[view], vmem.at[view], sem.at[c])

    @pl.loop(0, nch)
    def _(c):
        load(wg, wgv, wgsem, c, 1).start()
        load(wu, wuv, wusem, c, 1).start()

    @pl.loop(0, nch)
    def _(c):
        load(wd, wdv, wdsem, c, 0).start()

    barrier = pltpu.get_barrier_semaphore()

    @pl.loop(1, n)
    def _(i):
        pl.semaphore_signal(
            barrier, inc=1, device_id={"expert": lax.rem(me + i, n)}, device_id_type=MESH
        )

    pl.semaphore_signal(barrier, inc=1, device_id={"tensor": other}, device_id_type=MESH)

    srows = EXPERTS * SLOTS * PIECES
    r_i = iota((srows, PIECES * tok_dev), 0)
    c_i = iota((srows, PIECES * tok_dev), 1)
    same = r_i % PIECES == c_i // tok_dev
    pick = jnp.zeros((srows, PIECES * tok_dev), F32)
    r_c = iota((srows, 1), 0)
    scale = jnp.zeros((srows, 1), F32)
    for e in range(EXPERTS):
        for s in range(SLOTS):
            q = e * SLOTS + s
            live = jnp.where(s < counts[0, e], 1.0, 0.0).astype(F32)
            hit = same & (r_i // PIECES == q) & (c_i % tok_dev == slot[0, e, s])
            pick = jnp.where(hit, live, pick)
            scale = jnp.where(r_c // PIECES == q, gates[0, e, s], scale)
    pick = pick.astype(BF16)

    def stack(ref):
        wide = ref[...].astype(F32)
        parts = [wide[:, k * piece : (k + 1) * piece] for k in range(PIECES)]
        return jnp.concatenate(parts, axis=0).astype(BF16)

    xa = nn(pick, stack(tok))
    ga = nn(pick, stack(go))
    ga = ga * scale
    for e in range(EXPERTS):
        sendx[e] = xa[e * 16 : (e + 1) * 16].astype(BF16)
        sendg[e] = ga[e * 16 : (e + 1) * 16].astype(BF16)

    pl.semaphore_wait(barrier, n)

    def dispatch(buf, land, ssem, rsem, i, sending):
        peer = lax.rem(me + i, n)
        at = me if sending else peer
        return pltpu.make_async_remote_copy(
            src_ref=buf.at[peer // sub],
            dst_ref=land.at[at],
            send_sem=ssem.at[peer],
            recv_sem=rsem.at[at],
            device_id={"expert": peer},
            device_id_type=MESH,
        )

    @pl.loop(1, n)
    def _(i):
        dispatch(sendx, landx, xs, xv, i, True).start()

    @pl.loop(1, n)
    def _(i):
        dispatch(sendg, landg, gs, gv, i, True).start()

    landx[me] = sendx[me // sub]
    landg[me] = sendg[me // sub]

    d_r = iota((PIECES * rows, n * 16), 0)
    d_c = iota((PIECES * rows, n * 16), 1)
    spread = (d_c == (d_r % rows) * PIECES + d_r // rows).astype(F32).astype(BF16)
    m_r = iota((n * 16, 2 * RPIECES * rows), 0)
    m_c = iota((n * 16, 2 * RPIECES * rows), 1)
    m_row = (m_r // 16) * SLOTS + (m_r // RPIECES) % SLOTS
    m_part = ((m_r // 8) % 2) * RPIECES + m_r % RPIECES
    home[...] = (m_c == m_part * rows + m_row).astype(F32).astype(BF16)

    def unpack(land, out):
        moved = nn(spread, land[...].reshape(n * 16, piece)).astype(BF16)
        for k in range(PIECES):
            out[:, k * piece : (k + 1) * piece] = moved[k * rows : (k + 1) * rows]

    @pl.loop(1, n)
    def _(i):
        dispatch(sendx, landx, xs, xv, i, False).wait_recv()

    unpack(landx, xr)

    def swap(buf, land, ssem, rsem, c):
        return pltpu.make_async_remote_copy(
            src_ref=buf.at[c],
            dst_ref=land.at[c],
            send_sem=ssem.at[c],
            recv_sem=rsem.at[c],
            device_id={"tensor": other},
            device_id_type=MESH,
        )

    @pl.loop(0, nch)
    def _(c):
        at = pl.ds(pl.multiple_of(c * hc, hc), hc)
        load(wg, wgv, wgsem, c, 1).wait()
        gus[c, 0] = nn(xr[...], wgv[:, at])
        load(wu, wuv, wusem, c, 1).wait()
        gus[c, 1] = nn(xr[...], wuv[:, at])
        swap(gus, gur, guss, gurs, c).start()

    @pl.loop(1, n)
    def _(i):
        dispatch(sendg, landg, gs, gv, i, False).wait_recv()

    unpack(landg, gr)

    @pl.loop(0, nch)
    def _(c):
        at = pl.ds(pl.multiple_of(c * hc, hc), hc)
        load(wd, wdv, wdsem, c, 0).wait()
        ps[c] = nt(gr[...], wdv[at, :])
        swap(ps, pr, pss, prs, c).start()

    @pl.loop(0, nch)
    def _(c):
        at = pl.ds(pl.multiple_of(c * hc, hc), hc)
        swap(gus, gur, guss, gurs, c).wait_recv()
        swap(ps, pr, pss, prs, c).wait_recv()
        g = gus[c, 0] + gur[c, 0]
        u = gus[c, 1] + gur[c, 1]
        p = ps[c] + pr[c]
        sig = jax.nn.sigmoid(g)
        gsig = g * sig
        act[:, at] = (gsig * u).astype(BF16)
        dup[:, at] = (p * gsig).astype(BF16)
        dgt[:, at] = (p * u * sig * (1.0 + g * (1.0 - sig))).astype(BF16)

    def back(j, i, sending):
        peer = lax.rem(me + i, n)
        at = me if sending else peer
        return pltpu.make_async_remote_copy(
            src_ref=rets.at[j, peer],
            dst_ref=retl.at[j, at],
            send_sem=rss.at[j, peer],
            recv_sem=rrs.at[j, at],
            device_id={"expert": peer},
            device_id_type=MESH,
        )

    @pl.loop(0, nd)
    def _(j):
        at = pl.ds(pl.multiple_of(j * RCHUNK, RCHUNK), RCHUNK)
        y = nn(act[...], wdv[:, at])
        dx = nt(dgt[...], wgv[at, :]) + nt(dup[...], wuv[at, :])
        vals = (y.astype(BF16), dx.astype(BF16))
        parts = [v[:, k * rl : (k + 1) * rl] for v in vals for k in range(RPIECES)]
        total = nn(home[...], jnp.concatenate(parts, axis=0))
        rets[j] = total.astype(BF16).reshape(n, 16, rl)

        @pl.loop(1, n)
        def _(i):
            back(j, i, True).start()

        retl[j, me] = rets[j, me]

    tcol = iota((tok_dev, 1), 0)
    weights = []
    for e in range(EXPERTS):
        for s in range(SLOTS):
            live = jnp.where(s < counts[0, e], 1.0, 0.0).astype(F32)
            hit = jnp.where(tcol == slot[0, e, s], live, 0.0)
            weights.append((hit * gates[0, e, s], hit))

    @pl.loop(0, nd)
    def _(j):
        @pl.loop(1, n)
        def _(i):
            back(j, i, False).wait_recv()

        sums = []
        for e in range(EXPERTS):
            sums.append(
                lax.fori_loop(
                    1,
                    sub,
                    lambda d, acc: acc + retl[j, e * sub + d].astype(F32),
                    retl[j, e * sub].astype(F32),
                )
            )
        for arr, out in ((0, mixed), (1, gtok)):
            for k in range(RPIECES):
                acc = jnp.zeros((tok_dev, rl), F32)
                for e in range(EXPERTS):
                    for s in range(SLOTS):
                        row = arr * 8 + s * RPIECES + k
                        acc = acc + weights[e * SLOTS + s][arr] * sums[e][row : row + 1, :]
                out[:, pl.ds(pl.multiple_of(j * RCHUNK + k * rl, rl), rl)] = acc

    @pl.loop(1, n)
    def _(i):
        dispatch(sendx, landx, xs, xv, i, True).wait_send()
        dispatch(sendg, landg, gs, gv, i, True).wait_send()

        @pl.loop(0, nd)
        def _(j):
            back(j, i, True).wait_send()

    @pl.loop(0, nch)
    def _(c):
        swap(gus, gur, guss, gurs, c).wait_send()
        swap(ps, pr, pss, prs, c).wait_send()


def layer(n, tokens, grad_out, wg, wu, wd, counts, slot, gates):
    tok_dev, width = tokens.shape
    hl = wg.shape[1]
    hc = min(1024, hl)
    nch = hl // hc
    rows = n * SLOTS
    nd = width // RCHUNK
    rl = RCHUNK // RPIECES
    piece = width // PIECES
    vmem = pl.BlockSpec(memory_space=pltpu.VMEM)
    smem = pl.BlockSpec(memory_space=pltpu.SMEM)
    hbm = pl.BlockSpec(memory_space=pl.ANY)
    dma = pltpu.SemaphoreType.DMA
    return pl.pallas_call(
        functools.partial(layer_kernel, n, hl, hc),
        out_shape=(
            jax.ShapeDtypeStruct((rows, width), BF16),
            jax.ShapeDtypeStruct((rows, width), BF16),
            jax.ShapeDtypeStruct((rows, hl), BF16),
            jax.ShapeDtypeStruct((rows, hl), BF16),
            jax.ShapeDtypeStruct((rows, hl), BF16),
            jax.ShapeDtypeStruct((tok_dev, width), F32),
            jax.ShapeDtypeStruct((tok_dev, width), F32),
        ),
        in_specs=[vmem, vmem, hbm, hbm, hbm, smem, smem, smem],
        out_specs=(vmem,) * 7,
        scratch_shapes=[
            pltpu.VMEM((width, hl), BF16),
            pltpu.VMEM((width, hl), BF16),
            pltpu.VMEM((hl, width), BF16),
            pltpu.VMEM((n * 16, 2 * RPIECES * rows), BF16),
            pltpu.VMEM((EXPERTS, 16, piece), BF16),
            pltpu.VMEM((EXPERTS, 16, piece), BF16),
            pltpu.VMEM((n, 16, piece), BF16),
            pltpu.VMEM((n, 16, piece), BF16),
            pltpu.VMEM((nch, 2, rows, hc), F32),
            pltpu.VMEM((nch, 2, rows, hc), F32),
            pltpu.VMEM((nch, rows, hc), F32),
            pltpu.VMEM((nch, rows, hc), F32),
            pltpu.VMEM((nd, n, 16, rl), BF16),
            pltpu.VMEM((nd, n, 16, rl), BF16),
            dma((nch,)), dma((nch,)), dma((nch,)),
            dma((n,)), dma((n,)), dma((n,)), dma((n,)),
            dma((nch,)), dma((nch,)), dma((nch,)), dma((nch,)),
            dma((nd, n)), dma((nd, n)),
        ],
        compiler_params=pltpu.CompilerParams(
            collective_id=0, has_side_effects=True, vmem_limit_bytes=58 * 1024 * 1024
        ),
        name="layer",
    )(tokens, grad_out, wg, wu, wd, counts, slot, gates)


def grads_kernel(step_h, xr, gr, act, dup, dgt, mixed, gtok, m_out, t_out, gg, gu, gd):
    @pl.when(pl.program_id(0) == 0)
    def _():
        m_out[...] = mixed[...].astype(BF16)
        t_out[...] = gtok[...].astype(BF16)

    hl = dup.shape[1]
    x = xr[...]
    q = gr[...]
    for h in range(0, hl, step_h):
        gg[:, h : h + step_h] = tn(x, dgt[:, h : h + step_h]).astype(BF16)
        gu[:, h : h + step_h] = tn(x, dup[:, h : h + step_h]).astype(BF16)
        gd[h : h + step_h, :] = tn(act[:, h : h + step_h], q).astype(BF16)


def weight_grads(xr, gr, act, dup, dgt, mixed, gtok):
    rows, width = xr.shape
    hl = act.shape[1]
    tok_dev = mixed.shape[0]
    steps = 8
    dw = width // steps
    cols = pl.BlockSpec((rows, dw), lambda i: (0, i))
    hid = pl.BlockSpec((rows, hl), lambda i: (0, 0))
    small = pl.BlockSpec((tok_dev, width), lambda i: (0, 0))
    return pl.pallas_call(
        functools.partial(grads_kernel, min(256, hl)),
        grid=(steps,),
        out_shape=(
            jax.ShapeDtypeStruct((tok_dev, width), BF16),
            jax.ShapeDtypeStruct((tok_dev, width), BF16),
            jax.ShapeDtypeStruct((width, hl), BF16),
            jax.ShapeDtypeStruct((width, hl), BF16),
            jax.ShapeDtypeStruct((hl, width), BF16),
        ),
        in_specs=[cols, cols, hid, hid, hid, small, small],
        out_specs=(
            small,
            small,
            pl.BlockSpec((dw, hl), lambda i: (i, 0)),
            pl.BlockSpec((dw, hl), lambda i: (i, 0)),
            pl.BlockSpec((hl, dw), lambda i: (0, i)),
        ),
        compiler_params=pltpu.CompilerParams(
            dimension_semantics=("arbitrary",), vmem_limit_bytes=60 * 1024 * 1024
        ),
        name="weight_grads",
    )(xr, gr, act, dup, dgt, mixed, gtok)


def shards(tokens, grad_out, gate_weight, up_weight, down_weight, counts, slot_token, gates):
    n = lax.axis_size("expert")
    held = layer(
        n, tokens, grad_out, gate_weight, up_weight, down_weight, counts, slot_token, gates
    )
    return weight_grads(*held)


def solution(mesh):
    in_specs = (
        P(("groups", "expert"), "tensor"),
        P(("groups", "expert"), "tensor"),
        P("tensor", "expert"),
        P("tensor", "expert"),
        P("expert", "tensor"),
        P(("groups", "expert"), None),
        P(("groups", "expert"), None, None),
        P(("groups", "expert"), None, None),
    )
    out_specs = (
        P(("groups", "expert"), "tensor"),
        P(("groups", "expert"), "tensor"),
        P(("groups", "tensor"), "expert"),
        P(("groups", "tensor"), "expert"),
        P(("groups", "expert"), "tensor"),
    )
    return jax.shard_map(shards, mesh=mesh, in_specs=in_specs, out_specs=out_specs, check_vma=False)
```
